128 devices in a mesh: row: 8 (over y, x_hi), col: 16 (over z, x_lo, core).
Axes of the slice: x: 4 (x_hi: 2, x_lo: 2; x = x_hi * 2 + x_lo), y: 4, z: 4, core: 2. Of those that a mesh axis runs over, the one named last changes fastest.
Arguments:
- new_row: float32 [128, 192, 128], P('row', 'col'), may hold values from -4 to 4
- history: float32 [192, 192, 128, 128], P('row', 'col'), may hold values from -0.0390625 to 0.0390625
- hamiltonian: float32 [128, 128], replicated, may hold values from -0.5 to 0.5
Outputs:
- rows_out: float32 [3, 128, 192, 128], P(None, 'row', 'col')
The draws below stay inside these ranges and needn't reach their ends.
All inputs are finite; a program needn't handle non-finite values.
Results may differ from the reference program's by a relative error of at most 0.00026.
Values sent between devices are 32-bit elements; how exact they have to be, the bound alone decides.
A program may use at most 128 MiB of HBM per device.

```python
import jax
import jax.numpy as jnp
from jax import lax

NO = 128
STEPS = 3
NT = 192


def block_scale(own_key, extent, split, low, top_value):
    loudness, own = 1.0, jax.random.fold_in(own_key, 6)
    for position, shards_of in split:
        heights = jnp.exp(jax.random.uniform(jax.random.fold_in(own, position), (shards_of,), jnp.float32, low / len(split), top_value / len(split)))
        loudness = loudness * jnp.repeat(heights, extent[position] // shards_of).reshape([-1 if axis == position else 1 for axis in range(len(extent))])
    return loudness


def noise(stream_key, dims, width, bound, cuts=(), held_as=jnp.bfloat16):
    drawn = width * jax.random.normal(stream_key, dims, jnp.float32)
    if cuts:
        drawn = drawn * block_scale(stream_key, dims, cuts, -0.22, 0.18)
    return jnp.clip(drawn, -bound, bound).astype(held_as)


def setup_inputs(seed: int = 0) -> dict:
    streams_of = jax.random.split(jax.random.key(seed), 4)
    new_row = noise(streams_of[0], (NO, NT, NO), 0.7, 4.0, ((0, 8), (1, 16)), jnp.float32)
    history = noise(streams_of[1], (NT, NT, NO, NO), (NT * NO) ** -0.5, 0.0390625, ((0, 8), (1, 16)), jnp.float32)
    hamiltonian = noise(streams_of[2], (NO, NO), NO ** -0.5, 0.5, (), jnp.float32)
    return {"new_row": new_row, "history": history, "hamiltonian": hamiltonian}


time_step = 0.2


def reference(new_row, history, hamiltonian):
    current = new_row
    results = []
    for step_index in range(STEPS):
        sigma = current * current * current
        sigma_time = jnp.moveaxis(sigma, 1, 0)

        def accumulate(total, pair):
            sigma_tile, tiles = pair
            term = jnp.einsum("il,tlj->itj", sigma_tile, tiles, precision=lax.Precision.HIGHEST, preferred_element_type=jnp.float32)
            return total + term, None

        start_total = jnp.zeros(current.shape, jnp.float32)
        collision, unused = lax.scan(accumulate, start_total, (sigma_time, history))
        kinetic = jnp.einsum("itl,lj->itj", current, hamiltonian, precision=lax.Precision.HIGHEST, preferred_element_type=jnp.float32)
        current = current - time_step * (kinetic + collision)
        results.append(current)
    return jnp.stack(results)
```

```python
import jax
import jax.numpy as jnp
from jax import lax
from jax.experimental import pallas as pl
from jax.experimental.pallas import tpu as pltpu
from jax.sharding import PartitionSpec as P

STEPS = 3
time_step = 0.2
MESH = pl.DeviceIdType.MESH
bf16, f32 = jnp.bfloat16, jnp.float32
GROUP = 8
HALVES = 2
SUB = 8
TIMES = 12
ORB = 128
LANES = TIMES * ORB
DEPTH = 2 * LANES
PAIRS = TIMES // 2
SLOTS = 8
TILES = 24


def kernel(
    x_ref, ham_ref, hist_ref, out_ref,
    staged, hist_hi, hist_lo, operand, partial, arrived, sigma, mine, current,
    load_sem, sums_send, sums_recv, turn_send, turn_recv, wide_send, wide_recv, pair_send, pair_recv,
):
    row = lax.axis_index("row")
    col = lax.axis_index("col")
    chip = col // 2
    core = col % 2
    diagonal = row == chip
    off_diagonal = jnp.logical_not(diagonal)

    def load(tile):
        slot = lax.rem(tile, SLOTS)
        return pltpu.make_async_copy(hist_ref.at[tile], staged.at[slot], load_sem.at[slot])

    for tile in range(SLOTS):
        load(tile).start()

    def at(r, c, k):
        return (r, c * 2 + k)

    barrier = pltpu.get_barrier_semaphore()

    def greet(device):
        pl.semaphore_signal(barrier, inc=1, device_id=device, device_id_type=MESH)

    for m in range(1, GROUP):
        greet(at(lax.rem(row + m, GROUP), chip, core))
        greet(at(row, lax.rem(chip + m, GROUP), core))
    greet(at(row, chip, 1 - core))

    @pl.when(off_diagonal)
    def _():
        greet(at(chip, row, core))

    pl.semaphore_wait(barrier, 2 * (GROUP - 1) + 1 + jnp.where(diagonal, 0, 1))

    def rows_of(block):
        return pl.ds(pl.multiple_of(block * SUB, SUB), SUB)

    def turn(k, h):
        return pltpu.make_async_remote_copy(
            src_ref=mine.at[k, h],
            dst_ref=sigma.at[k, h, core, rows_of(row)],
            send_sem=turn_send.at[k, h],
            recv_sem=turn_recv.at[k, h],
            device_id=at(chip, row, core),
            device_id_type=MESH,
        )

    def start_turn(k, h):
        value = current[h]
        cubed = value * value * value

        @pl.when(off_diagonal)
        def _():
            mine[k, h] = cubed
            turn(k, h).start()

        @pl.when(diagonal)
        def _():
            sigma[k, h, core, rows_of(row)] = cubed

    def widen(k, h):
        @pl.when(off_diagonal)
        def _():
            turn(k, h).wait_recv()

        part = sigma.at[k, h, core, rows_of(chip)]
        for m in range(1, GROUP):
            pltpu.make_async_remote_copy(
                src_ref=part,
                dst_ref=part,
                send_sem=wide_send.at[k, h],
                recv_sem=wide_recv.at[k, h],
                device_id=at(row, lax.rem(chip + m, GROUP), core),
                device_id_type=MESH,
            ).start()

    def seven(k, h):
        return sigma.at[k, h, core, pl.ds(0, (GROUP - 1) * SUB)]

    def share(k, h):
        return pltpu.make_async_remote_copy(
            src_ref=sigma.at[k, h, core],
            dst_ref=sigma.at[k, h, core],
            send_sem=pair_send.at[k, h],
            recv_sem=pair_recv.at[k, h],
            device_id=at(row, chip, 1 - core),
            device_id_type=MESH,
        )

    def start_share(k, h):
        pltpu.make_async_copy(seven(k, h), seven(k, h), wide_recv.at[k, h]).wait()
        share(k, h).start()

    def split(tile, _):
        load(tile).wait()
        slot = lax.rem(tile, SLOTS)
        depth = pl.ds(pl.multiple_of(tile * ORB, ORB), ORB)

        def one(pair, _):
            for q in range(2):
                value = staged[slot, pair * 2 + q]
                hi = value.astype(bf16)
                lo = (value - hi.astype(f32)).astype(bf16)
                hist_hi[pair, depth, q * ORB:(q + 1) * ORB] = hi
                hist_lo[pair, depth, q * ORB:(q + 1) * ORB] = lo
            return 0

        lax.fori_loop(0, PAIRS, one, 0)

        @pl.when(tile + SLOTS < TILES)
        def _():
            load(tile + SLOTS).start()

        return 0

    def send_sums(k, h, lanes):
        for m in range(1, GROUP):
            other = lax.rem(row + m, GROUP)
            pltpu.make_async_remote_copy(
                src_ref=partial.at[k, h, rows_of(other), lanes],
                dst_ref=arrived.at[k, h, row, :, lanes],
                send_sem=sums_send.at[k, h],
                recv_sem=sums_recv.at[k, h],
                device_id=at(other, chip, core),
                device_id_type=MESH,
            ).start()

    def contract(k, h):
        share(k, h).wait_recv()
        for c in range(2):
            value = sigma[k, h, c]
            hi = value.astype(bf16)
            operand[0:64, c * LANES:(c + 1) * LANES] = hi
            operand[64:128, c * LANES:(c + 1) * LANES] = (value - hi.astype(f32)).astype(bf16)

        def one(pair, _):
            both = jnp.dot(operand[...], hist_hi[pair], preferred_element_type=f32)
            low = jnp.dot(operand[0:64], hist_lo[pair], preferred_element_type=f32)
            lanes = pl.ds(pl.multiple_of(pair * 256, 256), 256)
            partial[k, h, :, lanes] = both[0:64] + (both[64:128] + low)
            return 0

        lax.fori_loop(0, PAIRS // 2, one, 0)
        send_sums(k, h, pl.ds(0, LANES // 2))
        lax.fori_loop(PAIRS // 2, PAIRS, one, 0)
        send_sums(k, h, pl.ds(LANES // 2, LANES // 2))

    def advance(k, h):
        value = current[h]
        stacked = jnp.concatenate([value[:, t * ORB:(t + 1) * ORB] for t in range(TIMES)], axis=0)
        kinetic = jnp.dot(stacked, ham_ref[...], precision=lax.Precision.HIGHEST, preferred_element_type=f32)
        kinetic = jnp.concatenate([kinetic[t * SUB:(t + 1) * SUB] for t in range(TIMES)], axis=1)
        got = arrived.at[k, h, pl.ds(0, GROUP - 1)]
        pltpu.make_async_copy(got, got, sums_recv.at[k, h]).wait()
        total = partial[k, h, rows_of(row)]
        for m in range(1, GROUP):
            total += arrived[k, h, lax.rem(row + m, GROUP)]
        value = value - time_step * (kinetic + total)
        current[h] = value
        for t in range(TIMES):
            out_ref[k, t, h * SUB:(h + 1) * SUB] = value[:, t * ORB:(t + 1) * ORB]

    for h in range(HALVES):
        for t in range(TIMES):
            current[h, :, t * ORB:(t + 1) * ORB] = x_ref[t, h * SUB:(h + 1) * SUB]
        start_turn(0, h)
    lax.fori_loop(0, 8, split, 0)
    for h in range(HALVES):
        widen(0, h)
    lax.fori_loop(8, TILES, split, 0)
    start_share(0, 0)

    def step(k, _):
        start_share(k, 1)
        contract(k, 0)
        contract(k, 1)
        advance(k, 0)

        @pl.when(k < STEPS - 1)
        def _():
            start_turn(k + 1, 0)
            widen(k + 1, 0)

        advance(k, 1)

        @pl.when(k < STEPS - 1)
        def _():
            start_turn(k + 1, 1)
            widen(k + 1, 1)
            start_share(k + 1, 0)

        return 0

    lax.fori_loop(0, STEPS, step, 0)

    def drain(k, _):
        for h in range(HALVES):
            sent = partial.at[k, h, pl.ds(0, (GROUP - 1) * SUB)]
            pltpu.make_async_copy(sent, sent, sums_send.at[k, h]).wait()
            pltpu.make_async_copy(seven(k, h), seven(k, h), wide_send.at[k, h]).wait()
            share(k, h).wait_send()

            @pl.when(off_diagonal)
            def _():
                turn(k, h).wait_send()

        return 0

    lax.fori_loop(0, STEPS, drain, 0)


def per_device(new_row, history, hamiltonian):
    owned = jnp.transpose(new_row, (1, 0, 2))
    dma = pltpu.SemaphoreType.DMA
    out = pl.pallas_call(
        kernel,
        out_shape=jax.ShapeDtypeStruct((STEPS, TIMES, HALVES * SUB, ORB), f32),
        in_specs=[
            pl.BlockSpec(memory_space=pltpu.VMEM),
            pl.BlockSpec(memory_space=pltpu.VMEM),
            pl.BlockSpec(memory_space=pl.ANY),
        ],
        out_specs=pl.BlockSpec(memory_space=pltpu.VMEM),
        scratch_shapes=[
            pltpu.VMEM((SLOTS, TIMES, ORB, ORB), f32),
            pltpu.VMEM((PAIRS, DEPTH, 256), bf16),
            pltpu.VMEM((PAIRS, DEPTH, 256), bf16),
            pltpu.VMEM((128, DEPTH), bf16),
            pltpu.VMEM((STEPS, HALVES, GROUP * SUB, LANES), f32),
            pltpu.VMEM((STEPS, HALVES, GROUP, SUB, LANES), f32),
            pltpu.VMEM((STEPS, HALVES, 2, GROUP * SUB, LANES), f32),
            pltpu.VMEM((STEPS, HALVES, SUB, LANES), f32),
            pltpu.VMEM((HALVES, SUB, LANES), f32),
            dma((SLOTS,)),
        ] + [dma((STEPS, HALVES))] * 8,
        compiler_params=pltpu.CompilerParams(
            collective_id=0, has_side_effects=True, vmem_limit_bytes=56 << 20
        ),
        cost_estimate=pl.CostEstimate(flops=11_000_000_000, bytes_accessed=20_000_000, transcendentals=0),
    )(owned, hamiltonian, history)
    return jnp.transpose(out, (0, 2, 1, 3))


def solution(mesh):
    placed = (P("row", "col", None), P("row", "col", None, None), P())
    return jax.shard_map(
        per_device,
        mesh=mesh,
        in_specs=placed,
        out_specs=P(None, "row", "col", None),
        check_vma=False,
    )
```

```python
import jax
import jax.numpy as jnp
from jax import lax
from jax.experimental import pallas as pl
from jax.experimental.pallas import tpu as pltpu
from jax.sharding import PartitionSpec as P

STEPS = 3
time_step = 0.2
MESH = pl.DeviceIdType.MESH
bf16, f32 = jnp.bfloat16, jnp.float32
GROUP = 8
CHAINS = 2
CHUNKS = 2
SUB = 16 // CHAINS
ROWS = GROUP * SUB
TIMES = 12
ORB = 128
WIDE = TIMES * ORB // CHUNKS
DEPTH = 2 * TIMES * ORB
PER = TIMES // CHUNKS
PAIRS = TIMES // 2
SLOTS = 8
TILES = 24
UNROLL = 3
AFTER = 0
LATE = 14
EARLY = 8


def kernel(
    x_ref, ham_ref, hist_ref, out_ref,
    staged, hist_hi, hist_lo, operand, partial, arrived, sigma, mine, current,
    load_sem, sums_send, sums_recv, turn_send, turn_recv, wide_send, wide_recv, pair_send, pair_recv,
):
    row = lax.axis_index("row")
    col = lax.axis_index("col")
    chip = col // 2
    core = col % 2
    diagonal = row == chip
    off_diagonal = jnp.logical_not(diagonal)
    pieces = [(h, g) for h in range(CHAINS) for g in range(CHUNKS)]

    def load(tile):
        slot = lax.rem(tile, SLOTS)
        return pltpu.make_async_copy(hist_ref.at[tile], staged.at[slot], load_sem.at[slot])

    for tile in range(SLOTS):
        load(tile).start()

    def at(r, c, k):
        return (r, c * 2 + k)

    def remote(src, dst, send, recv, device):
        return pltpu.make_async_remote_copy(
            src_ref=src, dst_ref=dst, send_sem=send, recv_sem=recv, device_id=device, device_id_type=MESH
        )

    def wait_bytes(ref, sem):
        pltpu.make_async_copy(ref, ref, sem).wait()

    barrier = pltpu.get_barrier_semaphore()

    def greet(device):
        pl.semaphore_signal(barrier, inc=1, device_id=device, device_id_type=MESH)

    for m in range(1, GROUP):
        greet(at(lax.rem(row + m, GROUP), chip, core))
        greet(at(row, lax.rem(chip + m, GROUP), core))
    greet(at(row, chip, 1 - core))

    @pl.when(off_diagonal)
    def _():
        greet(at(chip, row, core))

    def rows_of(block, count=SUB):
        return pl.ds(pl.multiple_of(block * count, count), count)

    pl.semaphore_wait(barrier, 2 * (GROUP - 1) + 1 + jnp.where(diagonal, 0, 1))

    def turn(k, h, g):
        return remote(
            mine.at[k, h, g], sigma.at[k, h, g, core, rows_of(row)], turn_send.at[k, h, g], turn_recv.at[k, h, g],
            at(chip, row, core),
        )

    def start_turn(k, h, g):
        value = current[h, g]
        cubed = value * value * value

        @pl.when(off_diagonal)
        def _():
            mine[k, h, g] = cubed
            turn(k, h, g).start()

        @pl.when(diagonal)
        def _():
            sigma[k, h, g, core, rows_of(row)] = cubed

    def widen(k, h, g):
        pl.when(off_diagonal)(turn(k, h, g).wait_recv)
        part = sigma.at[k, h, g, core, rows_of(chip)]
        for m in range(1, GROUP):
            remote(
                part, part, wide_send.at[k, h, g], wide_recv.at[k, h, g], at(row, lax.rem(chip + m, GROUP), core)
            ).start()

    def most(k, h, g):
        return sigma.at[k, h, g, core, pl.ds(0, (GROUP - 1) * SUB)]

    def share(k, h, g):
        whole = sigma.at[k, h, g, core]
        return remote(whole, whole, pair_send.at[k, h, g], pair_recv.at[k, h, g], at(row, chip, 1 - core))

    def start_share(k, h, g):
        wait_bytes(most(k, h, g), wide_recv.at[k, h, g])
        share(k, h, g).start()

    def split(tile, _):
        load(tile).wait()
        slot = lax.rem(tile, SLOTS)
        half, time = tile // TIMES, tile % TIMES
        offset = (time // PER) * (2 * WIDE) + half * WIDE + (time % PER) * ORB
        depth = pl.ds(pl.multiple_of(offset, ORB), ORB)

        def one(pair, _):
            for q in range(2):
                value = staged[slot, pair * 2 + q]
                hi = value.astype(bf16)
                lo = (value - hi.astype(f32)).astype(bf16)
                hist_hi[pair, depth, q * ORB:(q + 1) * ORB] = hi
                hist_lo[pair, depth, q * ORB:(q + 1) * ORB] = lo
            return 0

        lax.fori_loop(0, PAIRS, one, 0)

        @pl.when(tile + SLOTS < TILES)
        def _():
            load(tile + SLOTS).start()

        return 0

    def send_sums(k, h, g):
        for m in range(1, GROUP):
            other = lax.rem(row + m, GROUP)
            remote(
                partial.at[k, h, g, rows_of(other)], arrived.at[k, h, g, row], sums_send.at[k, h, g],
                sums_recv.at[k, h, g], at(other, chip, core),
            ).start()

    def contract(k, h, between):
        for g in range(CHUNKS):
            share(k, h, g).wait_recv()
            for c in range(2):
                value = sigma[k, h, g, c]
                hi = value.astype(bf16)
                lanes = slice((2 * g + c) * WIDE, (2 * g + c + 1) * WIDE)
                operand[0:ROWS, lanes] = hi
                operand[ROWS:2 * ROWS, lanes] = (value - hi.astype(f32)).astype(bf16)
            depth = slice(2 * g * WIDE, 2 * (g + 1) * WIDE)

            def part(target):
                def one(p, _):
                    pair = target * (PER // 2) + p
                    both = jnp.dot(operand[:, depth], hist_hi[pair, depth], preferred_element_type=f32)
                    low = jnp.dot(operand[0:ROWS, depth], hist_lo[pair, depth], preferred_element_type=f32)
                    lanes = pl.ds(pl.multiple_of(p * 256, 256), 256)
                    total = both[0:ROWS] + (both[ROWS:2 * ROWS] + low)
                    if g > 0:
                        total += partial[k, h, target, :, lanes]
                    partial[k, h, target, :, lanes] = total
                    return 0

                lax.fori_loop(0, PER // 2, one, 0, unroll=UNROLL)

            if g < CHUNKS - 1:
                def every(target, _):
                    part(target)
                    return 0

                lax.fori_loop(0, CHUNKS, every, 0)
            else:
                for target in range(CHUNKS):
                    part(target)
                    send_sums(k, h, target)
                    between(target)

    def kinetic(value):
        stacked = jnp.concatenate([value[:, t * ORB:(t + 1) * ORB] for t in range(PER)], axis=0)
        moved = jnp.dot(stacked, ham_ref[...], precision=lax.Precision.HIGHEST, preferred_element_type=f32)
        return jnp.concatenate([moved[t * SUB:(t + 1) * SUB] for t in range(PER)], axis=1)

    def advance(k, h, g):
        value = current[h, g]
        moved = kinetic(value)
        wait_bytes(arrived.at[k, h, g, pl.ds(0, GROUP - 1)], sums_recv.at[k, h, g])
        total = partial[k, h, g, rows_of(row)]
        for m in range(1, GROUP):
            total += arrived[k, h, g, lax.rem(row + m, GROUP)]
        value = value - time_step * (moved + total)
        current[h, g] = value
        for t in range(PER):
            out_ref[k, g * PER + t, h * SUB:(h + 1) * SUB] = value[:, t * ORB:(t + 1) * ORB]

    for h, g in pieces:
        for t in range(PER):
            current[h, g, :, t * ORB:(t + 1) * ORB] = x_ref[g * PER + t, h * SUB:(h + 1) * SUB]
        start_turn(0, h, g)
    lax.fori_loop(0, EARLY, split, 0)
    for g in range(CHUNKS):
        widen(0, 0, g)
    lax.fori_loop(EARLY, LATE, split, 0)
    for g in range(CHUNKS):
        widen(0, 1, g)
    lax.fori_loop(LATE, TILES, split, 0)
    for g in range(CHUNKS):
        start_share(0, 0, g)

    def step(k, _):
        def between(target):
            if target == AFTER:
                for g in range(CHUNKS):
                    start_share(k, 1, g)

        contract(k, 0, between)
        contract(k, 1, lambda target: None)

        @pl.when(k < STEPS - 1)
        def _():
            for h in range(CHAINS):
                for g in range(CHUNKS):
                    advance(k, h, g)
                    start_turn(k + 1, h, g)
            for h in range(CHAINS):
                for g in range(CHUNKS):
                    widen(k + 1, h, g)
            for g in range(CHUNKS):
                start_share(k + 1, 0, g)

        @pl.when(k == STEPS - 1)
        def _():
            for h, g in pieces:
                advance(k, h, g)

        return 0

    lax.fori_loop(0, STEPS, step, 0)

    def drain(k, _):
        for h, g in pieces:
            wait_bytes(partial.at[k, h, g, pl.ds(0, (GROUP - 1) * SUB)], sums_send.at[k, h, g])
            wait_bytes(most(k, h, g), wide_send.at[k, h, g])
            share(k, h, g).wait_send()
            pl.when(off_diagonal)(turn(k, h, g).wait_send)
        return 0

    lax.fori_loop(0, STEPS, drain, 0)

def per_device(new_row, history, hamiltonian):
    dma = pltpu.SemaphoreType.DMA
    each = (CHAINS, CHUNKS)
    steps = (STEPS,) + each
    out = pl.pallas_call(
        kernel,
        out_shape=jax.ShapeDtypeStruct((STEPS, TIMES, 16, ORB), f32),
        in_specs=[
            pl.BlockSpec(memory_space=pltpu.VMEM),
            pl.BlockSpec(memory_space=pltpu.VMEM),
            pl.BlockSpec(memory_space=pl.ANY),
        ],
        out_specs=pl.BlockSpec(memory_space=pltpu.VMEM),
        scratch_shapes=[
            pltpu.VMEM((SLOTS, TIMES, ORB, ORB), f32),
            pltpu.VMEM((PAIRS, DEPTH, 256), bf16),
            pltpu.VMEM((PAIRS, DEPTH, 256), bf16),
            pltpu.VMEM((2 * ROWS, DEPTH), bf16),
            pltpu.VMEM(steps + (ROWS, WIDE), f32),
            pltpu.VMEM(steps + (GROUP, SUB, WIDE), f32),
            pltpu.VMEM(steps + (2, ROWS, WIDE), f32),
            pltpu.VMEM(steps + (SUB, WIDE), f32),
            pltpu.VMEM(each + (SUB, WIDE), f32),
            dma((SLOTS,)),
        ] + [dma(steps)] * 8,
        compiler_params=pltpu.CompilerParams(
            collective_id=0, has_side_effects=True, vmem_limit_bytes=58 << 20
        ),
        cost_estimate=pl.CostEstimate(flops=11_000_000_000, bytes_accessed=20_000_000, transcendentals=0),
    )(jnp.transpose(new_row, (1, 0, 2)), hamiltonian, history)
    return jnp.transpose(out, (0, 2, 1, 3))


def solution(mesh):
    placed = (P("row", "col", None), P("row", "col", None, None), P())
    return jax.shard_map(
        per_device,
        mesh=mesh,
        in_specs=placed,
        out_specs=P(None, "row", "col", None),
        check_vma=False,
    )
```

```python
import jax
import jax.numpy as jnp
from jax import lax
from jax.experimental import pallas as pl
from jax.experimental.pallas import tpu as pltpu
from jax.sharding import PartitionSpec as P

STEPS = 3
time_step = 0.2
MESH = pl.DeviceIdType.MESH
bf16, f32 = jnp.bfloat16, jnp.float32
GROUP = 8
CHAINS = 2
CHUNKS = 2
SUB = 16 // CHAINS
ROWS = GROUP * SUB
TIMES = 12
ORB = 128
WIDE = TIMES * ORB // CHUNKS
DEPTH = 2 * TIMES * ORB
PER = TIMES // CHUNKS
PAIRS = TIMES // 2
SLOTS = 8
TILES = 24
UNROLL = 3
LATE = 14
EARLY = 8


def kernel(
    x_ref, ham_ref, hist_ref, out_ref,
    staged, hist_hi, hist_lo, operand, partial, arrived, sigma, mine, current,
    load_sem, sums_send, sums_recv, turn_send, turn_recv, wide_send, wide_recv, pair_send, pair_recv,
):
    row = lax.axis_index("row")
    col = lax.axis_index("col")
    chip = col // 2
    core = col % 2
    diagonal = row == chip
    off_diagonal = jnp.logical_not(diagonal)
    pieces = [(h, g) for h in range(CHAINS) for g in range(CHUNKS)]

    def load(tile):
        slot = lax.rem(tile, SLOTS)
        return pltpu.make_async_copy(hist_ref.at[tile], staged.at[slot], load_sem.at[slot])

    for tile in range(SLOTS):
        load(tile).start()

    def at(r, c, k):
        return (r, c * 2 + k)

    def remote(src, dst, send, recv, device):
        return pltpu.make_async_remote_copy(
            src_ref=src, dst_ref=dst, send_sem=send, recv_sem=recv, device_id=device, device_id_type=MESH
        )

    def wait_bytes(ref, sem):
        pltpu.make_async_copy(ref, ref, sem).wait()

    barrier = pltpu.get_barrier_semaphore()

    def greet(device):
        pl.semaphore_signal(barrier, inc=1, device_id=device, device_id_type=MESH)

    for m in range(1, GROUP):
        greet(at(lax.rem(row + m, GROUP), chip, core))
        greet(at(row, lax.rem(chip + m, GROUP), core))
    greet(at(row, chip, 1 - core))

    @pl.when(off_diagonal)
    def _():
        greet(at(chip, row, core))

    def rows_of(block, count=SUB):
        return pl.ds(pl.multiple_of(block * count, count), count)

    for h, g in pieces:
        for t in range(PER):
            current[h, g, :, t * ORB:(t + 1) * ORB] = x_ref[g * PER + t, h * SUB:(h + 1) * SUB]

    pl.semaphore_wait(barrier, 2 * (GROUP - 1) + 1 + jnp.where(diagonal, 0, 1))

    def turn(k, h, g):
        return remote(
            mine.at[k, h, g], sigma.at[k, h, g, core, rows_of(row)], turn_send.at[k, h, g], turn_recv.at[k, h, g],
            at(chip, row, core),
        )

    def start_turn(k, h, g):
        value = current[h, g]
        cubed = value * value * value

        @pl.when(off_diagonal)
        def _():
            mine[k, h, g] = cubed
            turn(k, h, g).start()

        @pl.when(diagonal)
        def _():
            sigma[k, h, g, core, rows_of(row)] = cubed

    def widen(k, h, g):
        pl.when(off_diagonal)(turn(k, h, g).wait_recv)
        part = sigma.at[k, h, g, core, rows_of(chip)]
        for m in range(1, GROUP):
            remote(
                part, part, wide_send.at[k, h, g], wide_recv.at[k, h, g], at(row, lax.rem(chip + m, GROUP), core)
            ).start()

    def most(k, h, g):
        return sigma.at[k, h, g, core, pl.ds(0, (GROUP - 1) * SUB)]

    def share(k, h, g):
        whole = sigma.at[k, h, g, core]
        return remote(whole, whole, pair_send.at[k, h, g], pair_recv.at[k, h, g], at(row, chip, 1 - core))

    def start_share(k, h, g):
        wait_bytes(most(k, h, g), wide_recv.at[k, h, g])
        share(k, h, g).start()

    def split(tile, _):
        load(tile).wait()
        slot = lax.rem(tile, SLOTS)
        half, time = tile // TIMES, tile % TIMES
        offset = (time // PER) * (2 * WIDE) + half * WIDE + (time % PER) * ORB
        depth = pl.ds(pl.multiple_of(offset, ORB), ORB)

        def one(pair, _):
            for q in range(2):
                value = staged[slot, pair * 2 + q]
                hi = value.astype(bf16)
                lo = (value - hi.astype(f32)).astype(bf16)
                hist_hi[pair, depth, q * ORB:(q + 1) * ORB] = hi
                hist_lo[pair, depth, q * ORB:(q + 1) * ORB] = lo
            return 0

        lax.fori_loop(0, PAIRS, one, 0)

        @pl.when(tile + SLOTS < TILES)
        def _():
            load(tile + SLOTS).start()

        return 0

    def send_sums(k, h, g):
        for m in range(1, GROUP):
            other = lax.rem(row + m, GROUP)
            remote(
                partial.at[k, h, g, rows_of(other)], arrived.at[k, h, g, row], sums_send.at[k, h, g],
                sums_recv.at[k, h, g], at(other, chip, core),
            ).start()

    def contract(k, h, between):
        for g in range(CHUNKS):
            share(k, h, g).wait_recv()
            for c in range(2):
                value = sigma[k, h, g, c]
                hi = value.astype(bf16)
                lanes = slice((2 * g + c) * WIDE, (2 * g + c + 1) * WIDE)
                operand[0:ROWS, lanes] = hi
                operand[ROWS:2 * ROWS, lanes] = (value - hi.astype(f32)).astype(bf16)
            depth = slice(2 * g * WIDE, 2 * (g + 1) * WIDE)

            def part(target):
                def one(p, _):
                    pair = target * (PER // 2) + p
                    both = jnp.dot(operand[:, depth], hist_hi[pair, depth], preferred_element_type=f32)
                    low = jnp.dot(operand[0:ROWS, depth], hist_lo[pair, depth], preferred_element_type=f32)
                    lanes = pl.ds(pl.multiple_of(p * 256, 256), 256)
                    total = both[0:ROWS] + (both[ROWS:2 * ROWS] + low)
                    if g > 0:
                        total += partial[k, h, target, :, lanes]
                    partial[k, h, target, :, lanes] = total
                    return 0

                lax.fori_loop(0, PER // 2, one, 0, unroll=UNROLL)

            if g < CHUNKS - 1:
                def every(target, _):
                    part(target)
                    return 0

                lax.fori_loop(0, CHUNKS, every, 0)
            else:
                for target in range(CHUNKS):
                    part(target)
                    send_sums(k, h, target)
                    between(target)

    def kinetic(value):
        stacked = jnp.concatenate([value[:, t * ORB:(t + 1) * ORB] for t in range(PER)], axis=0)
        moved = jnp.dot(stacked, ham_ref[...], precision=lax.Precision.HIGHEST, preferred_element_type=f32)
        return jnp.concatenate([moved[t * SUB:(t + 1) * SUB] for t in range(PER)], axis=1)

    def advance(k, h, g):
        value = current[h, g]
        moved = kinetic(value)
        wait_bytes(arrived.at[k, h, g, pl.ds(0, GROUP - 1)], sums_recv.at[k, h, g])
        total = partial[k, h, g, rows_of(row)]
        for m in range(1, GROUP):
            total += arrived[k, h, g, lax.rem(row + m, GROUP)]
        value = value - time_step * (moved + total)
        current[h, g] = value
        for t in range(PER):
            out_ref[k, g * PER + t, h * SUB:(h + 1) * SUB] = value[:, t * ORB:(t + 1) * ORB]

    for h, g in pieces:
        start_turn(0, h, g)
    lax.fori_loop(0, EARLY, split, 0)
    for g in range(CHUNKS):
        widen(0, 0, g)
    lax.fori_loop(EARLY, LATE, split, 0)
    for g in range(CHUNKS):
        widen(0, 1, g)
    lax.fori_loop(LATE, TILES, split, 0)
    for g in range(CHUNKS):
        start_share(0, 0, g)

    def step(k, _):
        def between(target):
            start_share(k, 1, target)

        contract(k, 0, between)
        contract(k, 1, lambda target: None)

        @pl.when(k < STEPS - 1)
        def _():
            for h in range(CHAINS):
                for g in range(CHUNKS):
                    advance(k, h, g)
                    start_turn(k + 1, h, g)
            for h in range(CHAINS):
                for g in range(CHUNKS):
                    widen(k + 1, h, g)
            for g in range(CHUNKS):
                start_share(k + 1, 0, g)

        @pl.when(k == STEPS - 1)
        def _():
            for h, g in pieces:
                advance(k, h, g)

        return 0

    lax.fori_loop(0, STEPS, step, 0)

    def drain(k, _):
        for h, g in pieces:
            wait_bytes(partial.at[k, h, g, pl.ds(0, (GROUP - 1) * SUB)], sums_send.at[k, h, g])
            wait_bytes(most(k, h, g), wide_send.at[k, h, g])
            share(k, h, g).wait_send()
            pl.when(off_diagonal)(turn(k, h, g).wait_send)
        return 0

    lax.fori_loop(0, STEPS, drain, 0)

def per_device(new_row, history, hamiltonian):
    dma = pltpu.SemaphoreType.DMA
    each = (CHAINS, CHUNKS)
    steps = (STEPS,) + each
    out = pl.pallas_call(
        kernel,
        out_shape=jax.ShapeDtypeStruct((STEPS, TIMES, 16, ORB), f32),
        in_specs=[
            pl.BlockSpec(memory_space=pltpu.VMEM),
            pl.BlockSpec(memory_space=pltpu.VMEM),
            pl.BlockSpec(memory_space=pl.ANY),
        ],
        out_specs=pl.BlockSpec(memory_space=pltpu.VMEM),
        scratch_shapes=[
            pltpu.VMEM((SLOTS, TIMES, ORB, ORB), f32),
            pltpu.VMEM((PAIRS, DEPTH, 256), bf16),
            pltpu.VMEM((PAIRS, DEPTH, 256), bf16),
            pltpu.VMEM((2 * ROWS, DEPTH), bf16),
            pltpu.VMEM(steps + (ROWS, WIDE), f32),
            pltpu.VMEM(steps + (GROUP, SUB, WIDE), f32),
            pltpu.VMEM(steps + (2, ROWS, WIDE), f32),
            pltpu.VMEM(steps + (SUB, WIDE), f32),
            pltpu.VMEM(each + (SUB, WIDE), f32),
            dma((SLOTS,)),
        ] + [dma(steps)] * 8,
        compiler_params=pltpu.CompilerParams(
            collective_id=0, has_side_effects=True, vmem_limit_bytes=58 << 20
        ),
        cost_estimate=pl.CostEstimate(flops=11_000_000_000, bytes_accessed=20_000_000, transcendentals=0),
    )(jnp.transpose(new_row, (1, 0, 2)), hamiltonian, history)
    return jnp.transpose(out, (0, 2, 1, 3))


def solution(mesh):
    placed = (P("row", "col", None), P("row", "col", None, None), P())
    return jax.shard_map(
        per_device,
        mesh=mesh,
        in_specs=placed,
        out_specs=P(None, "row", "col", None),
        check_vma=False,
    )
```
